512 devices in a mesh: pairs: 128 (over x, z, y_hi, core), tm: 4 (over y_lo).
Axes of the slice: x: 4, y: 8 (y_hi: 2, y_lo: 4; y = y_hi * 4 + y_lo), z: 8, core: 2. Of those that a mesh axis runs over, the one named last changes fastest.
Arguments:
- records: bfloat16 [4, 512, 2048], P('tm', 'pairs'), may hold values from -50 to 50
- alive: int32 [512], P('pairs'), may hold values 0 or 1
- tile_block: int32 [128], P('pairs'), may hold values from 0 to 1
Outputs:
- stack: bfloat16 [512, 512, 256], P('tm', 'pairs')
The draws below stay inside these ranges and needn't reach their ends.
All inputs are finite; a program needn't handle non-finite values. No bound on the sum of `alive` on one device may be relied on, other than what follows from the above.
Results may differ from the reference program's by a relative error of at most 0.013.
Values may be sent and summed in bfloat16 or wider, within the bound.
No kernel may reach another device: no remote copies, remote signals or barrier semaphores. Data moves between devices by JAX's collectives and lax.ppermute only.
A program may use at most 64 MiB of HBM per device.

```python
import math
import jax
import jax.numpy as jnp
from jax import lax

CH_DEV = 4
SAMPLES = 2048
LAGS = 512
NBLK = 2
CHANNELS = 512
N_PAIRS = 128
N_TM = 4


def draw_records(key, part):
    key = jax.random.fold_in(key, 11)
    first, second, third = jax.random.split(key, 3)
    channels = CH_DEV * N_PAIRS
    chan_scale = jnp.exp(jax.random.uniform(second, (N_TM, channels, 1), jnp.float32) * math.log(10.0))
    time_scale = jnp.exp(jax.random.uniform(third, (N_TM, 1, SAMPLES), jnp.float32) * math.log(10.0))
    base = jnp.clip(jax.random.normal(first, (N_TM, channels, SAMPLES), jnp.float32), -4.5, 4.5)
    return (0.1 * base * chan_scale * time_scale).astype(jnp.bfloat16)


def with_ends(array, stream_key, smallest, largest):
    spot = [jax.random.randint(jax.random.fold_in(stream_key, axis), (), 0, length) for axis, length in enumerate(array.shape)]
    longest = array.shape.index(max(array.shape))
    next_to = spot[:longest] + [(spot[longest] + 1) % array.shape[longest]] + spot[longest + 1:]
    return array.at[tuple(spot)].set(smallest).at[tuple(next_to)].set(largest)


def setup_inputs(seed: int = 0) -> dict:
    key_list = jax.random.split(jax.random.key(seed), 4)
    records = draw_records(jax.random.fold_in(key_list[3], 71), 0)
    alive = with_ends((jax.random.randint(key_list[1], (CHANNELS,), 0, 8) < 7).astype(jnp.int32), jax.random.fold_in(key_list[1], 1), 0, 1)
    tile_block = with_ends(jax.random.randint(key_list[2], (N_PAIRS,), 0, NBLK), jax.random.fold_in(key_list[2], 1), 0, NBLK - 1).astype(jnp.int32)
    return {"records": records, "alive": alive, "tile_block": tile_block}


def normalize(records, alive):
    data = records.astype(jnp.float32)
    power = lax.optimization_barrier(jnp.mean(data * data, axis=-1, keepdims=True))
    scaled = data * lax.rsqrt(power + 1e-05) * alive[None, :, None].astype(jnp.float32)
    return scaled.astype(jnp.bfloat16)

def reference(records, alive, tile_block):
    normal = normalize(records, alive).astype(jnp.float32)
    segments = records.shape[0]
    channels = records.shape[1]
    samples = records.shape[2]
    rows = channels // N_PAIRS
    block_width = channels // NBLK
    length = 2 * samples
    spectra = jnp.fft.rfft(normal, n=length, axis=-1)
    half = LAGS // 2

    def one_tile(index):
        start = (index * rows).astype(jnp.int32)
        first = (tile_block[index] * block_width).astype(jnp.int32)
        own = lax.dynamic_slice_in_dim(spectra, start, rows, 1)
        cols = lax.dynamic_slice_in_dim(spectra, first, block_width, 1)
        product = jnp.conj(own)[:, :, None, :] * cols[:, None, :, :]
        circular = jnp.fft.irfft(product, n=length, axis=-1)
        lagged = jnp.concatenate([circular[..., length - half:], circular[..., :half]], axis=-1)
        rounded = lax.optimization_barrier(lagged.astype(jnp.bfloat16)).astype(jnp.float32)
        summed = lax.optimization_barrier(jnp.sum(rounded, axis=0)) / segments
        return jnp.transpose(summed, (2, 0, 1)).astype(jnp.bfloat16)
    tiles = lax.map(one_tile, jnp.arange(N_PAIRS, dtype=jnp.int32))
    return jnp.transpose(tiles, (1, 0, 2, 3)).reshape(LAGS, channels, block_width)
```

```python
import jax
import jax.numpy as jnp
from jax import lax
from jax.experimental import pallas as pl
from jax.experimental.pallas import tpu as pltpu
from jax.sharding import Mesh, PartitionSpec as P

LAGS = 512
NBLK = 2
HALF = LAGS // 2
PAIR_AXES = ("x", "z", "yh", "core")
SIZES = {"x": 4, "z": 8, "yh": 2, "core": 2}
MiB = 1 << 20


def normalize_kernel(records_ref, alive_ref, out_ref):
    data = records_ref[0].astype(jnp.float32)
    power = jnp.mean(data * data, axis=-1, keepdims=True)
    scaled = data * lax.rsqrt(power + 1e-05) * alive_ref[...].astype(jnp.float32)
    out_ref[...] = scaled.astype(jnp.bfloat16)


def normalize(records, alive):
    _, rows, samples = records.shape
    return pl.pallas_call(
        normalize_kernel,
        out_shape=jax.ShapeDtypeStruct((rows, samples), jnp.bfloat16),
        in_specs=[pl.BlockSpec(memory_space=pltpu.VMEM)] * 2,
        out_specs=pl.BlockSpec(memory_space=pltpu.VMEM),
        name="normalize",
    )(records, alive.reshape(rows, 1))


def correlate_kernel(where_ref, own_ref, mine_ref, other_ref, *rest):
    outs, skew = rest[:-1], rest[-1]
    rows, samples = own_ref.shape
    chunk = outs[0].shape[1]
    width = skew.shape[2]
    half = samples // 2
    block, core, seg = where_ref[0], where_ref[1], where_ref[2]
    count = len(outs)
    for c in range(rows):
        line = own_ref[pl.ds(c, 1), :].astype(jnp.float32)
        line = jnp.concatenate(
            [jnp.zeros((1, chunk), jnp.float32), line, jnp.zeros((1, width - samples - chunk), jnp.float32)], axis=1
        )
        grid = jnp.broadcast_to(line, (chunk, width))
        skew[c] = pltpu.roll(grid, 0, 1, stride=1, stride_axis=0).astype(jnp.bfloat16)
    cols = mine_ref.shape[0] // NBLK
    first = pl.multiple_of(block * cols, cols)
    near = mine_ref[pl.ds(first, cols), :]
    far = other_ref[pl.ds(first, cols), :]
    for step in range(count):
        part = lax.rem(seg + 1 + step, count)
        start = chunk * (count - 1 - part)
        near_at = pl.multiple_of(start + core * half, chunk)
        far_at = pl.multiple_of(start + (1 - core) * half, chunk)
        for c in range(rows):
            total = lax.dot_general(
                skew[c, :, pl.ds(near_at, half)], near, (((1,), (1,)), ((), ())), preferred_element_type=jnp.float32
            )
            total += lax.dot_general(
                skew[c, :, pl.ds(far_at, half)], far, (((1,), (1,)), ((), ())), preferred_element_type=jnp.float32
            )
            outs[step][c] = total.astype(jnp.bfloat16)


def correlate(where, own, mine, other, segments):
    rows, samples = own.shape
    chunk = LAGS // segments
    width = samples + (LAGS - chunk)
    cols = mine.shape[0] // NBLK
    shape = jax.ShapeDtypeStruct((rows, chunk, cols), jnp.bfloat16)
    return pl.pallas_call(
        correlate_kernel,
        out_shape=[shape] * segments,
        in_specs=[pl.BlockSpec(memory_space=pltpu.SMEM)] + [pl.BlockSpec(memory_space=pltpu.VMEM)] * 3,
        out_specs=[pl.BlockSpec(memory_space=pltpu.VMEM)] * segments,
        scratch_shapes=[pltpu.VMEM((rows, chunk, width), jnp.bfloat16)],
        compiler_params=pltpu.CompilerParams(vmem_limit_bytes=40 * MiB),
        cost_estimate=pl.CostEstimate(
            flops=2 * rows * LAGS * samples * cols, bytes_accessed=4 * MiB, transcendentals=0
        ),
        name="correlate",
    )(where, own, mine, other)


def local(records, alive, tile_block):
    segments = lax.axis_size("tm")
    core, seg = lax.axis_index("core"), lax.axis_index("tm")
    normal = normalize(records, alive)
    rows, samples = normal.shape
    half = samples // 2
    chip = lax.all_gather(normal, ("yh", "core"), axis=0, tiled=True)
    share = lax.dynamic_slice_in_dim(chip, core * half, half, 1)
    peers = SIZES["x"] * SIZES["z"]
    sent = jnp.broadcast_to(share[None], (peers,) + share.shape)
    got = lax.all_to_all(sent, ("x", "z"), 0, 0, tiled=True)
    mine = got.reshape(peers * share.shape[0], half)
    other = lax.ppermute(mine, "core", [(0, 1), (1, 0)])
    where = jnp.stack([tile_block[0], core, seg]).astype(jnp.int32)
    parts = correlate(where, normal, mine, other, segments)
    total = parts[-1].astype(jnp.float32)
    for step in range(segments - 1):
        pairs = [(i, (i + 1 + step) % segments) for i in range(segments)]
        total = total + lax.ppermute(parts[step], "tm", pairs).astype(jnp.float32)
    return jnp.transpose((total / segments).astype(jnp.bfloat16), (1, 0, 2))


def solution(mesh):
    shape = tuple(SIZES[a] for a in PAIR_AXES) + (mesh.shape["tm"],)
    fine = Mesh(mesh.devices.reshape(shape), PAIR_AXES + ("tm",))
    in_specs = (P("tm", PAIR_AXES, None), P(PAIR_AXES), P(PAIR_AXES))
    out_specs = P("tm", PAIR_AXES, None)
    return jax.shard_map(local, mesh=fine, in_specs=in_specs, out_specs=out_specs, check_vma=False)
```

```python
import jax
import jax.numpy as jnp
from jax import lax
from jax.experimental import pallas as pl
from jax.experimental.pallas import tpu as pltpu
from jax.sharding import Mesh, PartitionSpec as P

LAGS = 512
NBLK = 2
PAIR_AXES = ("x", "z", "yh", "core")
SIZES = {"x": 4, "z": 8, "yh": 2, "core": 2}
MiB = 1 << 20
SMEM = pl.BlockSpec(memory_space=pltpu.SMEM)
VMEM = pl.BlockSpec(memory_space=pltpu.VMEM)


def normalize_kernel(records_ref, alive_ref, out_ref):
    data = records_ref[0].astype(jnp.float32)
    power = jnp.mean(data * data, axis=-1, keepdims=True)
    row = lax.broadcasted_iota(jnp.int32, power.shape, 0)
    alive = jnp.zeros(power.shape, jnp.float32)
    for c in range(data.shape[0]):
        alive = jnp.where(row == c, alive_ref[c].astype(jnp.float32), alive)
    out_ref[...] = (data * lax.rsqrt(power + 1e-05) * alive).astype(jnp.bfloat16)


def normalize(records, alive):
    _, rows, samples = records.shape
    return pl.pallas_call(
        normalize_kernel,
        out_shape=jax.ShapeDtypeStruct((rows, samples), jnp.bfloat16),
        in_specs=[VMEM, SMEM],
        out_specs=VMEM,
        name="normalize",
    )(records, alive)


def correlate_kernel(rows, where_ref, own_ref, mine_ref, other_ref, *rest):
    out_refs, skew_ref = rest[:-1], rest[-1]
    samples, width = own_ref.shape[1], skew_ref.shape[1]
    chunk = skew_ref.shape[0] // rows
    cols, half = mine_ref.shape[0] // NBLK, mine_ref.shape[1]
    last = (width - samples) // chunk
    block, core = where_ref[0], where_ref[1]
    for c in range(rows):
        line = own_ref[pl.ds(c, 1), :].astype(jnp.float32)
        line = jnp.concatenate(
            [jnp.zeros((1, chunk), jnp.float32), line, jnp.zeros((1, width - samples - chunk), jnp.float32)], axis=1
        )
        grid = jnp.broadcast_to(line, (chunk, width))
        skewed = pltpu.roll(grid, 0, 1, stride=1, stride_axis=0)
        skew_ref[pl.ds(c * chunk, chunk), :] = skewed.astype(jnp.bfloat16)
    first = pl.multiple_of(block * cols, cols)
    for i, out_ref in enumerate(out_refs):
        start = chunk * (last - where_ref[2 + i])
        total = 0.0
        for at, ref in ((core, mine_ref), (1 - core, other_ref)):
            window = pl.ds(pl.multiple_of(start + at * half, chunk), half)
            total += lax.dot_general(
                skew_ref[:, window], ref[pl.ds(first, cols), :], (((1,), (1,)), ((), ())),
                preferred_element_type=jnp.float32,
            )
        out_ref[...] = total.astype(jnp.bfloat16).reshape(out_ref.shape)


def correlate(where, own, mine, other):
    rows, samples = own.shape
    count = where.shape[0] - 2
    chunk = LAGS // count
    width = samples + LAGS - chunk
    cols = mine.shape[0] // NBLK
    shape = jax.ShapeDtypeStruct((rows, chunk, cols), jnp.bfloat16)
    return pl.pallas_call(
        lambda *refs: correlate_kernel(rows, *refs),
        out_shape=[shape] * count,
        in_specs=[SMEM, VMEM, VMEM, VMEM],
        out_specs=[VMEM] * count,
        scratch_shapes=[pltpu.VMEM((rows * chunk, width), jnp.bfloat16)],
        compiler_params=pltpu.CompilerParams(vmem_limit_bytes=40 * MiB),
        cost_estimate=pl.CostEstimate(
            flops=2 * rows * LAGS * samples * cols, bytes_accessed=4 * MiB, transcendentals=0
        ),
        name="correlate",
    )(where, own, mine, other)


def local(records, alive, tile_block):
    segments = lax.axis_size("tm")
    core, seg = lax.axis_index("core"), lax.axis_index("tm")
    normal = normalize(records, alive)
    rows, samples = normal.shape
    half = samples // 2
    chip = lax.all_gather(normal, "core", axis=0, tiled=True)
    share = lax.dynamic_slice_in_dim(chip, core * half, half, 1)
    for axes in (("z", "yh"), ("x",)):
        peers = 1
        for axis in axes:
            peers *= SIZES[axis]
        sent = jnp.broadcast_to(share[None], (peers,) + share.shape)
        share = lax.all_to_all(sent, axes, 0, 0, tiled=True).reshape(peers * share.shape[0], half)
    other = lax.ppermute(share, "core", [(0, 1), (1, 0)])
    shifts = (2, 1, 3, 0)
    owners = [lax.rem(seg + shift, segments) for shift in shifts]
    where = jnp.stack([tile_block[0], core] + owners).astype(jnp.int32)
    terms = correlate(where, normal, share, other)
    total = terms[-1].astype(jnp.float32)
    for shift, term in zip(shifts[:-1], terms):
        term = lax.ppermute(term, "tm", [(i, (i + shift) % segments) for i in range(segments)])
        total = total + term.astype(jnp.float32)
    return jnp.transpose((total / segments).astype(jnp.bfloat16), (1, 0, 2))


def solution(mesh):
    shape = tuple(SIZES[a] for a in PAIR_AXES) + (mesh.shape["tm"],)
    fine = Mesh(mesh.devices.reshape(shape), PAIR_AXES + ("tm",))
    in_specs = (P("tm", PAIR_AXES, None), P(PAIR_AXES), P(PAIR_AXES))
    out_specs = P("tm", PAIR_AXES, None)
    return jax.shard_map(local, mesh=fine, in_specs=in_specs, out_specs=out_specs, check_vma=False)
```

```python
import jax
import jax.numpy as jnp
from jax import lax
from jax.experimental import pallas as pl
from jax.experimental.pallas import tpu as pltpu
from jax.sharding import Mesh, PartitionSpec as P

LAGS = 512
NBLK = 2
PAIR_AXES = ("x", "z", "yh", "core")
SIZES = {"x": 4, "z": 8, "yh": 2, "core": 2}
MiB = 1 << 20
SMEM = pl.BlockSpec(memory_space=pltpu.SMEM)
VMEM = pl.BlockSpec(memory_space=pltpu.VMEM)


def normalize_kernel(records_ref, alive_ref, out_ref, copies_ref):
    data = records_ref[0].astype(jnp.float32)
    power = jnp.mean(data * data, axis=-1, keepdims=True)
    row = lax.broadcasted_iota(jnp.int32, power.shape, 0)
    alive = jnp.zeros(power.shape, jnp.float32)
    for c in range(data.shape[0]):
        alive = jnp.where(row == c, alive_ref[c].astype(jnp.float32), alive)
    normal = (data * lax.rsqrt(power + 1e-05) * alive).astype(jnp.bfloat16)
    out_ref[...] = normal
    for i in range(copies_ref.shape[0]):
        copies_ref[i] = normal


def normalize(records, alive, copies):
    _, rows, samples = records.shape
    return pl.pallas_call(
        normalize_kernel,
        out_shape=[
            jax.ShapeDtypeStruct((rows, samples), jnp.bfloat16),
            jax.ShapeDtypeStruct((copies, rows, samples), jnp.bfloat16),
        ],
        in_specs=[VMEM, SMEM],
        out_specs=[VMEM, VMEM],
        name="normalize",
    )(records, alive)


def correlate_kernel(rows, where_ref, own_ref, mine_ref, other_ref, *rest):
    out_refs, skew_ref, cols_ref = rest[:-2], rest[-2], rest[-1]
    samples, width = own_ref.shape[1], skew_ref.shape[1]
    chunk = skew_ref.shape[0] // rows
    cols = cols_ref.shape[0]
    half = cols // 2
    last = (width - samples) // chunk
    block, core = where_ref[0], where_ref[1]
    for c in range(rows):
        line = own_ref[pl.ds(c, 1), :].astype(jnp.float32)
        line = jnp.concatenate(
            [jnp.zeros((1, chunk), jnp.float32), line, jnp.zeros((1, width - samples - chunk), jnp.float32)], axis=1
        )
        grid = jnp.broadcast_to(line, (chunk, width))
        skewed = pltpu.roll(grid, 0, 1, stride=1, stride_axis=0)
        skew_ref[pl.ds(c * chunk, chunk), :] = skewed.astype(jnp.bfloat16)
    first = block * half
    group = 2 * rows
    upper = lax.broadcasted_iota(jnp.int32, (group, samples), 0) < rows
    for at in range(0, half, 2 * group):
        here = pl.ds(pl.multiple_of(first + at, 2 * group), 2 * group)
        near, far = mine_ref[here, :].astype(jnp.float32), other_ref[here, :].astype(jnp.float32)
        even, odd = jnp.where(core == 0, near, far), jnp.where(core == 0, far, near)
        woven = []
        for part in range(2):
            e, o = even[part * group : (part + 1) * group], odd[part * group : (part + 1) * group]
            woven += [jnp.where(upper, e, pltpu.roll(o, rows, 0)), jnp.where(upper, pltpu.roll(e, rows, 0), o)]
        cols_ref[pl.ds(2 * at, 4 * group), :] = jnp.concatenate(woven, axis=0).astype(jnp.bfloat16)
    for i, out_ref in enumerate(out_refs):
        window = pl.ds(pl.multiple_of(chunk * (last - where_ref[2 + i]), chunk), samples)
        total = lax.dot_general(
            skew_ref[:, window], cols_ref[...], (((1,), (1,)), ((), ())), preferred_element_type=jnp.float32
        )
        out_ref[...] = total.astype(jnp.bfloat16).reshape(out_ref.shape)


def correlate(where, own, mine, other):
    rows, samples = own.shape
    count = where.shape[0] - 2
    chunk = LAGS // count
    width = samples + LAGS - chunk
    cols = 2 * mine.shape[0] // NBLK
    shape = jax.ShapeDtypeStruct((rows, chunk, cols), jnp.bfloat16)
    return pl.pallas_call(
        lambda *refs: correlate_kernel(rows, *refs),
        out_shape=[shape] * count,
        in_specs=[SMEM, VMEM, VMEM, VMEM],
        out_specs=[VMEM] * count,
        scratch_shapes=[pltpu.VMEM((rows * chunk, width), jnp.bfloat16), pltpu.VMEM((cols, samples), jnp.bfloat16)],
        compiler_params=pltpu.CompilerParams(vmem_limit_bytes=40 * MiB),
        cost_estimate=pl.CostEstimate(
            flops=2 * rows * LAGS * samples * cols, bytes_accessed=4 * MiB, transcendentals=0
        ),
        name="correlate",
    )(where, own, mine, other)


def local(records, alive, tile_block):
    segments = lax.axis_size("tm")
    core, seg = lax.axis_index("core"), lax.axis_index("tm")
    normal, sent = normalize(records, alive, SIZES["z"] * SIZES["yh"])
    slab = lax.all_to_all(sent, ("z", "yh"), 0, 0, tiled=True).reshape(-1, sent.shape[2])
    sent = jnp.broadcast_to(slab[None], (SIZES["x"],) + slab.shape)
    share = lax.all_to_all(sent, "x", 0, 0, tiled=True).reshape(-1, slab.shape[1])
    other = lax.ppermute(share, "core", [(0, 1), (1, 0)])
    shifts = (2, 1, 3, 0)
    owners = [lax.rem(seg + shift, segments) for shift in shifts]
    where = jnp.stack([tile_block[0], core] + owners).astype(jnp.int32)
    terms = correlate(where, normal, share, other)
    total = terms[-1].astype(jnp.float32)
    for shift, term in zip(shifts[:-1], terms):
        term = lax.ppermute(term, "tm", [(i, (i + shift) % segments) for i in range(segments)])
        total = total + term.astype(jnp.float32)
    return jnp.transpose((total / segments).astype(jnp.bfloat16), (1, 0, 2))


def solution(mesh):
    shape = tuple(SIZES[a] for a in PAIR_AXES) + (mesh.shape["tm"],)
    fine = Mesh(mesh.devices.reshape(shape), PAIR_AXES + ("tm",))
    in_specs = (P("tm", PAIR_AXES, None), P(PAIR_AXES), P(PAIR_AXES))
    out_specs = P("tm", PAIR_AXES, None)
    return jax.shard_map(local, mesh=fine, in_specs=in_specs, out_specs=out_specs, check_vma=False)
```

```python
import jax
import jax.numpy as jnp
from jax import lax
from jax.experimental import pallas as pl
from jax.experimental.pallas import tpu as pltpu
from jax.sharding import Mesh, PartitionSpec as P

LAGS = 512
NBLK = 2
PAIR_AXES = ("x", "z", "yh", "core")
SIZES = {"x": 4, "z": 8, "yh": 2, "core": 2}
MiB = 1 << 20
SENDS = ((3, 2, 1, 0), (2, 0, 3, 1), (1, 3, 0, 2), (0, 1, 2, 3))
SMEM = pl.BlockSpec(memory_space=pltpu.SMEM)
VMEM = pl.BlockSpec(memory_space=pltpu.VMEM)


def normalize_kernel(records_ref, alive_ref, out_ref, copies_ref):
    data = records_ref[0].astype(jnp.float32)
    power = jnp.mean(data * data, axis=-1, keepdims=True)
    row = lax.broadcasted_iota(jnp.int32, power.shape, 0)
    alive = jnp.zeros(power.shape, jnp.float32)
    for c in range(data.shape[0]):
        alive = jnp.where(row == c, alive_ref[c].astype(jnp.float32), alive)
    normal = (data * lax.rsqrt(power + 1e-05) * alive).astype(jnp.bfloat16)
    out_ref[...] = normal
    for i in range(copies_ref.shape[0]):
        copies_ref[i] = normal


def normalize(records, alive, copies):
    _, rows, samples = records.shape
    return pl.pallas_call(
        normalize_kernel,
        out_shape=[
            jax.ShapeDtypeStruct((rows, samples), jnp.bfloat16),
            jax.ShapeDtypeStruct((copies, rows, samples), jnp.bfloat16),
        ],
        in_specs=[VMEM, SMEM],
        out_specs=[VMEM, VMEM],
        name="normalize",
    )(records, alive)


def correlate_kernel(rows, where_ref, own_ref, mine_ref, other_ref, *rest):
    out_refs, skew_ref, cols_ref = rest[:-2], rest[-2], rest[-1]
    samples, width = own_ref.shape[1], skew_ref.shape[1]
    chunk = skew_ref.shape[0] // rows
    cols = cols_ref.shape[0]
    half = cols // 2
    last = (width - samples) // chunk
    block, core = where_ref[0], where_ref[1]
    for c in range(rows):
        line = own_ref[pl.ds(c, 1), :].astype(jnp.float32)
        line = jnp.concatenate(
            [jnp.zeros((1, chunk), jnp.float32), line, jnp.zeros((1, width - samples - chunk), jnp.float32)], axis=1
        )
        grid = jnp.broadcast_to(line, (chunk, width))
        skewed = pltpu.roll(grid, 0, 1, stride=1, stride_axis=0)
        skew_ref[pl.ds(c * chunk, chunk), :] = skewed.astype(jnp.bfloat16)
    first = block * half
    group = 2 * rows
    upper = lax.broadcasted_iota(jnp.int32, (group, samples), 0) < rows
    for at in range(0, half, 2 * group):
        here = pl.ds(pl.multiple_of(first + at, 2 * group), 2 * group)
        near, far = mine_ref[here, :].astype(jnp.float32), other_ref[here, :].astype(jnp.float32)
        even, odd = jnp.where(core == 0, near, far), jnp.where(core == 0, far, near)
        woven = []
        for part in range(2):
            e, o = even[part * group : (part + 1) * group], odd[part * group : (part + 1) * group]
            woven += [jnp.where(upper, e, pltpu.roll(o, rows, 0)), jnp.where(upper, pltpu.roll(e, rows, 0), o)]
        cols_ref[pl.ds(2 * at, 4 * group), :] = jnp.concatenate(woven, axis=0).astype(jnp.bfloat16)
    for i, out_ref in enumerate(out_refs):
        window = pl.ds(pl.multiple_of(chunk * (last - where_ref[2 + i]), chunk), samples)
        total = lax.dot_general(
            skew_ref[:, window], cols_ref[...], (((1,), (1,)), ((), ())), preferred_element_type=jnp.float32
        )
        out_ref[...] = total.astype(jnp.bfloat16).reshape(out_ref.shape)


def correlate(where, own, mine, other):
    rows, samples = own.shape
    count = where.shape[0] - 2
    chunk = LAGS // count
    width = samples + LAGS - chunk
    cols = 2 * mine.shape[0] // NBLK
    shape = jax.ShapeDtypeStruct((rows, chunk, cols), jnp.bfloat16)
    return pl.pallas_call(
        lambda *refs: correlate_kernel(rows, *refs),
        out_shape=[shape] * count,
        in_specs=[SMEM, VMEM, VMEM, VMEM],
        out_specs=[VMEM] * count,
        scratch_shapes=[pltpu.VMEM((rows * chunk, width), jnp.bfloat16), pltpu.VMEM((cols, samples), jnp.bfloat16)],
        compiler_params=pltpu.CompilerParams(vmem_limit_bytes=40 * MiB),
        cost_estimate=pl.CostEstimate(
            flops=2 * rows * LAGS * samples * cols, bytes_accessed=4 * MiB, transcendentals=0
        ),
        name="correlate",
    )(where, own, mine, other)


def local(records, alive, tile_block):
    segments = lax.axis_size("tm")
    core, seg = lax.axis_index("core"), lax.axis_index("tm")
    normal, sent = normalize(records, alive, SIZES["z"] * SIZES["yh"])
    slab = lax.all_to_all(sent, ("z", "yh"), 0, 0, tiled=True).reshape(-1, sent.shape[2])
    sent = jnp.broadcast_to(slab[None], (SIZES["x"],) + slab.shape)
    share = lax.all_to_all(sent, "x", 0, 0, tiled=True).reshape(-1, slab.shape[1])
    other = lax.ppermute(share, "core", [(0, 1), (1, 0)])
    sends = []
    for column in zip(*SENDS):
        value = column[-1]
        for i in reversed(range(segments - 1)):
            value = jnp.where(seg == i, column[i], value)
        sends.append(value)
    where = jnp.stack([tile_block[0], core] + sends).astype(jnp.int32)
    near, turned, later, own = correlate(where, normal, share, other)
    inner = (seg == 1) | (seg == 2)
    turned = lax.ppermute(turned, "tm", [(0, 2), (3, 1), (1, 0), (2, 3)])
    passed = lax.ppermute(near, "tm", [(0, 1), (3, 2)])
    passed = jnp.where(inner, passed.astype(jnp.float32), 0.0)
    middle = lax.ppermute(near, "tm", [(1, 2), (2, 1)])
    later = (later.astype(jnp.float32) + passed).astype(jnp.bfloat16)
    last = lax.ppermute(later, "tm", [(0, 1), (3, 2), (1, 3), (2, 0)])
    total = own.astype(jnp.float32) + turned.astype(jnp.float32) + last.astype(jnp.float32)
    total = total + jnp.where(inner, middle.astype(jnp.float32), 0.0)
    return jnp.transpose((total / segments).astype(jnp.bfloat16), (1, 0, 2))


def solution(mesh):
    shape = tuple(SIZES[a] for a in PAIR_AXES) + (mesh.shape["tm"],)
    fine = Mesh(mesh.devices.reshape(shape), PAIR_AXES + ("tm",))
    in_specs = (P("tm", PAIR_AXES, None), P(PAIR_AXES), P(PAIR_AXES))
    out_specs = P("tm", PAIR_AXES, None)
    return jax.shard_map(local, mesh=fine, in_specs=in_specs, out_specs=out_specs, check_vma=False)
```

```python
import jax
import jax.numpy as jnp
from jax import lax
from jax.experimental import pallas as pl
from jax.experimental.pallas import tpu as pltpu
from jax.sharding import Mesh, PartitionSpec as P

LAGS = 512
NBLK = 2
PAIR_AXES = ("x", "z", "yh", "core")
SIZES = {"x": 4, "z": 8, "yh": 2, "core": 2}
MiB = 1 << 20
SENDS = ((3, 2, 1, 0), (2, 0, 3, 1), (1, 3, 0, 2), (0, 1, 2, 3))
SMEM = pl.BlockSpec(memory_space=pltpu.SMEM)
VMEM = pl.BlockSpec(memory_space=pltpu.VMEM)


def normalize_kernel(records_ref, alive_ref, out_ref, copies_ref):
    data = records_ref[0].astype(jnp.float32)
    power = jnp.mean(data * data, axis=-1, keepdims=True)
    row = lax.broadcasted_iota(jnp.int32, power.shape, 0)
    alive = jnp.zeros(power.shape, jnp.float32)
    for c in range(data.shape[0]):
        alive = jnp.where(row == c, alive_ref[c].astype(jnp.float32), alive)
    normal = (data * lax.rsqrt(power + 1e-05) * alive).astype(jnp.bfloat16)
    out_ref[...] = normal
    for i in range(copies_ref.shape[0]):
        copies_ref[i] = normal


def normalize(records, alive, copies):
    _, rows, samples = records.shape
    return pl.pallas_call(
        normalize_kernel,
        out_shape=[
            jax.ShapeDtypeStruct((rows, samples), jnp.bfloat16),
            jax.ShapeDtypeStruct((copies, rows, samples), jnp.bfloat16),
        ],
        in_specs=[VMEM, SMEM],
        out_specs=[VMEM, VMEM],
        name="normalize",
    )(records, alive)


def correlate_kernel(rows, where_ref, own_ref, mine_ref, other_ref, *rest):
    out_refs, skew_ref, cols_ref = rest[:-2], rest[-2], rest[-1]
    samples, width = own_ref.shape[1], skew_ref.shape[1]
    chunk = skew_ref.shape[0] // rows
    cols = cols_ref.shape[0]
    half = cols // 2
    last = (width - samples) // chunk
    block, core = where_ref[0], where_ref[1]
    for c in range(rows):
        line = own_ref[pl.ds(c, 1), :].astype(jnp.float32)
        line = jnp.concatenate(
            [jnp.zeros((1, chunk), jnp.float32), line, jnp.zeros((1, width - samples - chunk), jnp.float32)], axis=1
        )
        grid = jnp.broadcast_to(line, (chunk, width))
        skewed = pltpu.roll(grid, 0, 1, stride=1, stride_axis=0)
        skew_ref[pl.ds(c * chunk, chunk), :] = skewed.astype(jnp.bfloat16)
    first = block * half
    group = 2 * rows
    upper = lax.broadcasted_iota(jnp.int32, (group, samples), 0) < rows
    for at in range(0, half, 2 * group):
        here = pl.ds(pl.multiple_of(first + at, 2 * group), 2 * group)
        near, far = mine_ref[here, :].astype(jnp.float32), other_ref[here, :].astype(jnp.float32)
        even, odd = jnp.where(core == 0, near, far), jnp.where(core == 0, far, near)
        woven = []
        for part in range(2):
            e, o = even[part * group : (part + 1) * group], odd[part * group : (part + 1) * group]
            woven += [jnp.where(upper, e, pltpu.roll(o, rows, 0)), jnp.where(upper, pltpu.roll(e, rows, 0), o)]
        cols_ref[pl.ds(2 * at, 4 * group), :] = jnp.concatenate(woven, axis=0).astype(jnp.bfloat16)
    for i, out_ref in enumerate(out_refs):
        window = pl.ds(pl.multiple_of(chunk * (last - where_ref[2 + i]), chunk), samples)
        total = lax.dot_general(
            skew_ref[:, window], cols_ref[...], (((1,), (1,)), ((), ())), preferred_element_type=jnp.float32
        )
        out_ref[...] = total.astype(jnp.bfloat16).reshape(out_ref.shape)


def correlate(where, segments, own, mine, other):
    rows, samples = own.shape
    count = where.shape[0] - 2
    chunk = LAGS // segments
    width = samples + LAGS - chunk
    cols = 2 * mine.shape[0] // NBLK
    shape = jax.ShapeDtypeStruct((rows, chunk, cols), jnp.bfloat16)
    return pl.pallas_call(
        lambda *refs: correlate_kernel(rows, *refs),
        out_shape=[shape] * count,
        in_specs=[SMEM, VMEM, VMEM, VMEM],
        out_specs=[VMEM] * count,
        scratch_shapes=[pltpu.VMEM((rows * chunk, width), jnp.bfloat16), pltpu.VMEM((cols, samples), jnp.bfloat16)],
        compiler_params=pltpu.CompilerParams(vmem_limit_bytes=40 * MiB),
        cost_estimate=pl.CostEstimate(
            flops=2 * rows * count * chunk * samples * cols, bytes_accessed=4 * MiB, transcendentals=0
        ),
        name="correlate",
    )(where, own, mine, other)


def local(records, alive, tile_block):
    segments = lax.axis_size("tm")
    core, seg = lax.axis_index("core"), lax.axis_index("tm")
    normal, sent = normalize(records, alive, SIZES["z"] * SIZES["yh"])
    slab = lax.all_to_all(sent, ("z", "yh"), 0, 0, tiled=True).reshape(-1, sent.shape[2])
    sent = jnp.broadcast_to(slab[None], (SIZES["x"],) + slab.shape)
    share = lax.all_to_all(sent, "x", 0, 0, tiled=True).reshape(-1, slab.shape[1])
    other = lax.ppermute(share, "core", [(0, 1), (1, 0)])
    sends = []
    for column in zip(*SENDS):
        value = column[-1]
        for i in reversed(range(segments - 1)):
            value = jnp.where(seg == i, column[i], value)
        sends.append(value)
    early = jnp.stack([tile_block[0], core] + sends[:2]).astype(jnp.int32)
    late = jnp.stack([tile_block[0], core] + sends[2:]).astype(jnp.int32)
    near, turned = correlate(early, segments, normal, share, other)
    later, own = correlate(late, segments, normal, share, other)
    inner = (seg == 1) | (seg == 2)
    turned = lax.ppermute(turned, "tm", [(0, 2), (3, 1), (1, 0), (2, 3)])
    passed = lax.ppermute(near, "tm", [(0, 1), (3, 2)])
    passed = jnp.where(inner, passed.astype(jnp.float32), 0.0)
    middle = lax.ppermute(near, "tm", [(1, 2), (2, 1)])
    later = (later.astype(jnp.float32) + passed).astype(jnp.bfloat16)
    last = lax.ppermute(later, "tm", [(0, 1), (3, 2), (1, 3), (2, 0)])
    total = own.astype(jnp.float32) + turned.astype(jnp.float32) + last.astype(jnp.float32)
    total = total + jnp.where(inner, middle.astype(jnp.float32), 0.0)
    return jnp.transpose((total / segments).astype(jnp.bfloat16), (1, 0, 2))


def solution(mesh):
    shape = tuple(SIZES[a] for a in PAIR_AXES) + (mesh.shape["tm"],)
    fine = Mesh(mesh.devices.reshape(shape), PAIR_AXES + ("tm",))
    in_specs = (P("tm", PAIR_AXES, None), P(PAIR_AXES), P(PAIR_AXES))
    out_specs = P("tm", PAIR_AXES, None)
    return jax.shard_map(local, mesh=fine, in_specs=in_specs, out_specs=out_specs, check_vma=False)
```

```python
import jax
import jax.numpy as jnp
from jax import lax
from jax.experimental import pallas as pl
from jax.experimental.pallas import tpu as pltpu
from jax.sharding import Mesh, PartitionSpec as P

LAGS = 512
NBLK = 2
PAIR_AXES = ("x", "z", "yh", "core")
SIZES = {"x": 4, "z": 8, "yh": 2, "core": 2}
MiB = 1 << 20
SENDS = ((3, 2, 1, 0), (2, 0, 3, 1), (1, 3, 0, 2), (0, 1, 2, 3))
SMEM = pl.BlockSpec(memory_space=pltpu.SMEM)
VMEM = pl.BlockSpec(memory_space=pltpu.VMEM)


def normalize_kernel(records_ref, alive_ref, out_ref, copies_ref):
    data = records_ref[0].astype(jnp.float32)
    power = jnp.mean(data * data, axis=-1, keepdims=True)
    row = lax.broadcasted_iota(jnp.int32, power.shape, 0)
    alive = jnp.zeros(power.shape, jnp.float32)
    for c in range(data.shape[0]):
        alive = jnp.where(row == c, alive_ref[c].astype(jnp.float32), alive)
    normal = (data * lax.rsqrt(power + 1e-05) * alive).astype(jnp.bfloat16)
    out_ref[...] = normal
    for i in range(copies_ref.shape[0]):
        copies_ref[i] = normal


def normalize(records, alive, copies):
    _, rows, samples = records.shape
    return pl.pallas_call(
        normalize_kernel,
        out_shape=[
            jax.ShapeDtypeStruct((rows, samples), jnp.bfloat16),
            jax.ShapeDtypeStruct((copies, rows, samples), jnp.bfloat16),
        ],
        in_specs=[VMEM, SMEM],
        out_specs=[VMEM, VMEM],
        name="normalize",
    )(records, alive)


def correlate_kernel(rows, where_ref, own_ref, mine_ref, other_ref, *rest):
    out_refs, skew_ref, cols_ref = rest[:-2], rest[-2], rest[-1]
    samples, width = own_ref.shape[1], skew_ref.shape[1]
    chunk = skew_ref.shape[0] // rows
    cols = cols_ref.shape[0]
    half = cols // 2
    last = (width - samples) // chunk
    block, core = where_ref[0], where_ref[1]
    for c in range(rows):
        line = own_ref[pl.ds(c, 1), :].astype(jnp.float32)
        line = jnp.concatenate(
            [jnp.zeros((1, chunk), jnp.float32), line, jnp.zeros((1, width - samples - chunk), jnp.float32)], axis=1
        )
        grid = jnp.broadcast_to(line, (chunk, width))
        skewed = pltpu.roll(grid, 0, 1, stride=1, stride_axis=0)
        skew_ref[pl.ds(c * chunk, chunk), :] = skewed.astype(jnp.bfloat16)
    first = block * half
    group = 2 * rows
    upper = lax.broadcasted_iota(jnp.int32, (group, samples), 0) < rows
    for at in range(0, half, 2 * group):
        here = pl.ds(pl.multiple_of(first + at, 2 * group), 2 * group)
        near, far = mine_ref[here, :].astype(jnp.float32), other_ref[here, :].astype(jnp.float32)
        even, odd = jnp.where(core == 0, near, far), jnp.where(core == 0, far, near)
        woven = []
        for part in range(2):
            e, o = even[part * group : (part + 1) * group], odd[part * group : (part + 1) * group]
            woven += [jnp.where(upper, e, pltpu.roll(o, rows, 0)), jnp.where(upper, pltpu.roll(e, rows, 0), o)]
        cols_ref[pl.ds(2 * at, 4 * group), :] = jnp.concatenate(woven, axis=0).astype(jnp.bfloat16)
    for i, out_ref in enumerate(out_refs):
        window = pl.ds(pl.multiple_of(chunk * (last - where_ref[2 + i]), chunk), samples)
        total = lax.dot_general(
            skew_ref[:, window], cols_ref[...], (((1,), (1,)), ((), ())), preferred_element_type=jnp.float32
        )
        out_ref[...] = total.astype(jnp.bfloat16).reshape(out_ref.shape)


def correlate(where, segments, own, mine, other):
    rows, samples = own.shape
    count = where.shape[0] - 2
    chunk = LAGS // segments
    width = samples + LAGS - chunk
    cols = 2 * mine.shape[0] // NBLK
    shape = jax.ShapeDtypeStruct((rows, chunk, cols), jnp.bfloat16)
    return pl.pallas_call(
        lambda *refs: correlate_kernel(rows, *refs),
        out_shape=[shape] * count,
        in_specs=[SMEM, VMEM, VMEM, VMEM],
        out_specs=[VMEM] * count,
        scratch_shapes=[pltpu.VMEM((rows * chunk, width), jnp.bfloat16), pltpu.VMEM((cols, samples), jnp.bfloat16)],
        compiler_params=pltpu.CompilerParams(vmem_limit_bytes=40 * MiB),
        cost_estimate=pl.CostEstimate(
            flops=2 * rows * count * chunk * samples * cols, bytes_accessed=4 * MiB, transcendentals=0
        ),
        name="correlate",
    )(where, own, mine, other)


def local(records, alive, tile_block):
    segments = lax.axis_size("tm")
    core, seg = lax.axis_index("core"), lax.axis_index("tm")
    normal, sent = normalize(records, alive, SIZES["z"] * SIZES["yh"])
    slab = lax.all_to_all(sent, ("z", "yh"), 0, 0, tiled=True).reshape(-1, sent.shape[2])
    sent = jnp.broadcast_to(slab[None], (SIZES["x"],) + slab.shape)
    share = lax.all_to_all(sent, "x", 0, 0, tiled=True).reshape(-1, slab.shape[1])
    other = lax.ppermute(share, "core", [(0, 1), (1, 0)])
    sends = []
    for column in zip(*SENDS):
        value = column[-1]
        for i in reversed(range(segments - 1)):
            value = jnp.where(seg == i, column[i], value)
        sends.append(value)
    early = jnp.stack([tile_block[0], core] + sends[:1]).astype(jnp.int32)
    middling = jnp.stack([tile_block[0], core] + sends[1:2]).astype(jnp.int32)
    late = jnp.stack([tile_block[0], core] + sends[2:]).astype(jnp.int32)
    (near,) = correlate(early, segments, normal, share, other)
    (turned,) = correlate(middling, segments, normal, share, other)
    later, own = correlate(late, segments, normal, share, other)
    inner = (seg == 1) | (seg == 2)
    turned = lax.ppermute(turned, "tm", [(0, 2), (3, 1), (1, 0), (2, 3)])
    passed = lax.ppermute(near, "tm", [(0, 1), (3, 2)])
    passed = jnp.where(inner, passed.astype(jnp.float32), 0.0)
    middle = lax.ppermute(near, "tm", [(1, 2), (2, 1)])
    later = (later.astype(jnp.float32) + passed).astype(jnp.bfloat16)
    last = lax.ppermute(later, "tm", [(0, 1), (3, 2), (1, 3), (2, 0)])
    total = own.astype(jnp.float32) + turned.astype(jnp.float32) + last.astype(jnp.float32)
    total = total + jnp.where(inner, middle.astype(jnp.float32), 0.0)
    return jnp.transpose((total / segments).astype(jnp.bfloat16), (1, 0, 2))


def solution(mesh):
    shape = tuple(SIZES[a] for a in PAIR_AXES) + (mesh.shape["tm"],)
    fine = Mesh(mesh.devices.reshape(shape), PAIR_AXES + ("tm",))
    in_specs = (P("tm", PAIR_AXES, None), P(PAIR_AXES), P(PAIR_AXES))
    out_specs = P("tm", PAIR_AXES, None)
    return jax.shard_map(local, mesh=fine, in_specs=in_specs, out_specs=out_specs, check_vma=False)
```

```python
import jax
import jax.numpy as jnp
from jax import lax
from jax.experimental import pallas as pl
from jax.experimental.pallas import tpu as pltpu
from jax.sharding import Mesh, PartitionSpec as P

LAGS = 512
NBLK = 2
PAIR_AXES = ("x", "z", "yh", "core")
SIZES = {"x": 4, "z": 8, "yh": 2, "core": 2}
MiB = 1 << 20
SENDS = ((3, 2, 1, 0), (2, 0, 3, 1), (1, 3, 0, 2), (0, 1, 2, 3))
SMEM = pl.BlockSpec(memory_space=pltpu.SMEM)
VMEM = pl.BlockSpec(memory_space=pltpu.VMEM)


def normalize_kernel(records_ref, alive_ref, out_ref, copies_ref):
    data = records_ref[0].astype(jnp.float32)
    power = jnp.mean(data * data, axis=-1, keepdims=True)
    row = lax.broadcasted_iota(jnp.int32, power.shape, 0)
    alive = jnp.zeros(power.shape, jnp.float32)
    for c in range(data.shape[0]):
        alive = jnp.where(row == c, alive_ref[c].astype(jnp.float32), alive)
    normal = (data * lax.rsqrt(power + 1e-05) * alive).astype(jnp.bfloat16)
    out_ref[...] = normal
    for i in range(copies_ref.shape[0]):
        copies_ref[i] = normal


def normalize(records, alive, copies):
    _, rows, samples = records.shape
    return pl.pallas_call(
        normalize_kernel,
        out_shape=[
            jax.ShapeDtypeStruct((rows, samples), jnp.bfloat16),
            jax.ShapeDtypeStruct((copies, rows, samples), jnp.bfloat16),
        ],
        in_specs=[VMEM, SMEM],
        out_specs=[VMEM, VMEM],
        name="normalize",
    )(records, alive)


def correlate_kernel(rows, where_ref, own_ref, mine_ref, other_ref, *rest):
    out_refs, skew_ref, cols_ref = rest[:-2], rest[-2], rest[-1]
    samples, width = own_ref.shape[1], skew_ref.shape[1]
    chunk = skew_ref.shape[0] // rows
    cols = cols_ref.shape[0]
    half = cols // 2
    last = (width - samples) // chunk
    block, core = where_ref[0], where_ref[1]
    for c in range(rows):
        line = own_ref[pl.ds(c, 1), :].astype(jnp.float32)
        line = jnp.concatenate(
            [jnp.zeros((1, chunk), jnp.float32), line, jnp.zeros((1, width - samples - chunk), jnp.float32)], axis=1
        )
        grid = jnp.broadcast_to(line, (chunk, width))
        skewed = pltpu.roll(grid, 0, 1, stride=1, stride_axis=0)
        skew_ref[pl.ds(c * chunk, chunk), :] = skewed.astype(jnp.bfloat16)
    first = block * half
    group = 2 * rows
    upper = lax.broadcasted_iota(jnp.int32, (group, samples), 0) < rows
    for at in range(0, half, 2 * group):
        here = pl.ds(pl.multiple_of(first + at, 2 * group), 2 * group)
        near, far = mine_ref[here, :].astype(jnp.float32), other_ref[here, :].astype(jnp.float32)
        even, odd = jnp.where(core == 0, near, far), jnp.where(core == 0, far, near)
        woven = []
        for part in range(2):
            e, o = even[part * group : (part + 1) * group], odd[part * group : (part + 1) * group]
            woven += [jnp.where(upper, e, pltpu.roll(o, rows, 0)), jnp.where(upper, pltpu.roll(e, rows, 0), o)]
        cols_ref[pl.ds(2 * at, 4 * group), :] = jnp.concatenate(woven, axis=0).astype(jnp.bfloat16)
    for i, out_ref in enumerate(out_refs):
        window = pl.ds(pl.multiple_of(chunk * (last - where_ref[2 + i]), chunk), samples)
        total = lax.dot_general(
            skew_ref[:, window], cols_ref[...], (((1,), (1,)), ((), ())), preferred_element_type=jnp.float32
        )
        out_ref[...] = total.astype(jnp.bfloat16).reshape(out_ref.shape)


def correlate(where, segments, own, mine, other):
    rows, samples = own.shape
    count = where.shape[0] - 2
    chunk = LAGS // segments
    width = samples + LAGS - chunk
    cols = 2 * mine.shape[0] // NBLK
    shape = jax.ShapeDtypeStruct((rows, chunk, cols), jnp.bfloat16)
    return pl.pallas_call(
        lambda *refs: correlate_kernel(rows, *refs),
        out_shape=[shape] * count,
        in_specs=[SMEM, VMEM, VMEM, VMEM],
        out_specs=[VMEM] * count,
        scratch_shapes=[pltpu.VMEM((rows * chunk, width), jnp.bfloat16), pltpu.VMEM((cols, samples), jnp.bfloat16)],
        compiler_params=pltpu.CompilerParams(vmem_limit_bytes=40 * MiB),
        cost_estimate=pl.CostEstimate(
            flops=2 * rows * count * chunk * samples * cols, bytes_accessed=4 * MiB, transcendentals=0
        ),
        name="correlate",
    )(where, own, mine, other)


def local(records, alive, tile_block):
    segments = lax.axis_size("tm")
    core, seg = lax.axis_index("core"), lax.axis_index("tm")
    normal, sent = normalize(records, alive, SIZES["z"] * SIZES["yh"])
    slab = lax.all_to_all(sent, ("z", "yh"), 0, 0, tiled=True).reshape(-1, sent.shape[2])
    sent = jnp.broadcast_to(slab[None], (SIZES["x"],) + slab.shape)
    share = lax.all_to_all(sent, "x", 0, 0, tiled=True).reshape(-1, slab.shape[1])
    other = lax.ppermute(share, "core", [(0, 1), (1, 0)])
    sends = []
    for column in zip(*SENDS):
        value = column[-1]
        for i in reversed(range(segments - 1)):
            value = jnp.where(seg == i, column[i], value)
        sends.append(value)
    def chunks(*owners):
        where = jnp.stack([tile_block[0], core] + list(owners)).astype(jnp.int32)
        return correlate(where, segments, normal, share, other)

    (near,) = chunks(*sends[0:1])
    (turned,) = chunks(*sends[1:2])
    (later,) = chunks(*sends[2:3])
    (own,) = chunks(*sends[3:4])
    inner = (seg == 1) | (seg == 2)
    turned = lax.ppermute(turned, "tm", [(0, 2), (3, 1), (1, 0), (2, 3)])
    passed = lax.ppermute(near, "tm", [(0, 1), (3, 2)])
    passed = jnp.where(inner, passed.astype(jnp.float32), 0.0)
    middle = lax.ppermute(near, "tm", [(1, 2), (2, 1)])
    later = (later.astype(jnp.float32) + passed).astype(jnp.bfloat16)
    last = lax.ppermute(later, "tm", [(0, 1), (3, 2), (1, 3), (2, 0)])
    total = own.astype(jnp.float32) + turned.astype(jnp.float32) + last.astype(jnp.float32)
    total = total + jnp.where(inner, middle.astype(jnp.float32), 0.0)
    return jnp.transpose((total / segments).astype(jnp.bfloat16), (1, 0, 2))


def solution(mesh):
    shape = tuple(SIZES[a] for a in PAIR_AXES) + (mesh.shape["tm"],)
    fine = Mesh(mesh.devices.reshape(shape), PAIR_AXES + ("tm",))
    in_specs = (P("tm", PAIR_AXES, None), P(PAIR_AXES), P(PAIR_AXES))
    out_specs = P("tm", PAIR_AXES, None)
    return jax.shard_map(local, mesh=fine, in_specs=in_specs, out_specs=out_specs, check_vma=False)
```

```python
import jax
import jax.numpy as jnp
from jax import lax
from jax.experimental import pallas as pl
from jax.experimental.pallas import tpu as pltpu
from jax.sharding import Mesh, PartitionSpec as P

LAGS = 512
NBLK = 2
PAIR_AXES = ("x", "z", "yh", "core")
SIZES = {"x": 4, "z": 8, "yh": 2, "core": 2}
MiB = 1 << 20
SENDS = ((3, 2, 1, 0), (2, 0, 3, 1), (1, 3, 0, 2), (0, 1, 2, 3))
SMEM = pl.BlockSpec(memory_space=pltpu.SMEM)
VMEM = pl.BlockSpec(memory_space=pltpu.VMEM)


def normalize_kernel(records_ref, alive_ref, out_ref, copies_ref):
    data = records_ref[0].astype(jnp.float32)
    power = jnp.mean(data * data, axis=-1, keepdims=True)
    row = lax.broadcasted_iota(jnp.int32, power.shape, 0)
    alive = jnp.zeros(power.shape, jnp.float32)
    for c in range(data.shape[0]):
        alive = jnp.where(row == c, alive_ref[c].astype(jnp.float32), alive)
    normal = (data * lax.rsqrt(power + 1e-05) * alive).astype(jnp.bfloat16)
    out_ref[...] = normal
    for i in range(copies_ref.shape[0]):
        copies_ref[i] = normal


def normalize(records, alive, copies):
    _, rows, samples = records.shape
    return pl.pallas_call(
        normalize_kernel,
        out_shape=[
            jax.ShapeDtypeStruct((rows, samples), jnp.bfloat16),
            jax.ShapeDtypeStruct((copies, rows, samples), jnp.bfloat16),
        ],
        in_specs=[VMEM, SMEM],
        out_specs=[VMEM, VMEM],
        name="normalize",
    )(records, alive)


def correlate_kernel(rows, where_ref, own_ref, mine_ref, other_ref, *rest):
    out_ref, line_ref, skew_ref, cols_ref = rest
    samples = own_ref.shape[1]
    chunk = skew_ref.shape[0] // rows
    cols = cols_ref.shape[0]
    half = cols // 2
    last = LAGS // chunk - 1
    block, core = where_ref[0], where_ref[1]
    start = pl.multiple_of(chunk * (last - where_ref[2]), chunk)
    line_ref[...] = jnp.zeros(line_ref.shape, jnp.float32)
    line_ref[:, pl.ds(2 * chunk, samples)] = own_ref[...].astype(jnp.float32)
    for c in range(rows):
        line = line_ref[pl.ds(c, 1), pl.ds(start, samples + chunk)]
        grid = jnp.broadcast_to(line, (chunk, samples + chunk))
        skewed = pltpu.roll(grid, 0, 1, stride=1, stride_axis=0)
        skew_ref[pl.ds(c * chunk, chunk), :] = skewed[:, chunk:].astype(jnp.bfloat16)
    first = block * half
    group = 2 * rows
    upper = lax.broadcasted_iota(jnp.int32, (group, samples), 0) < rows
    for at in range(0, half, 2 * group):
        here = pl.ds(pl.multiple_of(first + at, 2 * group), 2 * group)
        near, far = mine_ref[here, :].astype(jnp.float32), other_ref[here, :].astype(jnp.float32)
        even, odd = jnp.where(core == 0, near, far), jnp.where(core == 0, far, near)
        woven = []
        for part in range(2):
            e, o = even[part * group : (part + 1) * group], odd[part * group : (part + 1) * group]
            woven += [jnp.where(upper, e, pltpu.roll(o, rows, 0)), jnp.where(upper, pltpu.roll(e, rows, 0), o)]
        cols_ref[pl.ds(2 * at, 4 * group), :] = jnp.concatenate(woven, axis=0).astype(jnp.bfloat16)
    total = lax.dot_general(
        skew_ref[...], cols_ref[...], (((1,), (1,)), ((), ())), preferred_element_type=jnp.float32
    )
    out_ref[...] = total.astype(jnp.bfloat16).reshape(out_ref.shape)


def correlate(where, segments, own, mine, other):
    rows, samples = own.shape
    chunk = LAGS // segments
    cols = 2 * mine.shape[0] // NBLK
    return pl.pallas_call(
        lambda *refs: correlate_kernel(rows, *refs),
        out_shape=jax.ShapeDtypeStruct((rows, chunk, cols), jnp.bfloat16),
        in_specs=[SMEM, VMEM, VMEM, VMEM],
        out_specs=VMEM,
        scratch_shapes=[
            pltpu.VMEM((rows, samples + LAGS), jnp.float32),
            pltpu.VMEM((rows * chunk, samples), jnp.bfloat16),
            pltpu.VMEM((cols, samples), jnp.bfloat16),
        ],
        compiler_params=pltpu.CompilerParams(vmem_limit_bytes=40 * MiB),
        cost_estimate=pl.CostEstimate(
            flops=2 * rows * chunk * samples * cols, bytes_accessed=4 * MiB, transcendentals=0
        ),
        name="correlate",
    )(where, own, mine, other)


def local(records, alive, tile_block):
    segments = lax.axis_size("tm")
    core, seg = lax.axis_index("core"), lax.axis_index("tm")
    normal, sent = normalize(records, alive, SIZES["z"] * SIZES["yh"])
    slab = lax.all_to_all(sent, ("z", "yh"), 0, 0, tiled=True).reshape(-1, sent.shape[2])
    sent = jnp.broadcast_to(slab[None], (SIZES["x"],) + slab.shape)
    share = lax.all_to_all(sent, "x", 0, 0, tiled=True).reshape(-1, slab.shape[1])
    other = lax.ppermute(share, "core", [(0, 1), (1, 0)])
    sends = []
    for column in zip(*SENDS):
        value = column[-1]
        for i in reversed(range(segments - 1)):
            value = jnp.where(seg == i, column[i], value)
        sends.append(value)
    near, turned, later, own = (
        correlate(jnp.stack([tile_block[0], core, owner]).astype(jnp.int32), segments, normal, share, other)
        for owner in sends
    )
    inner = (seg == 1) | (seg == 2)
    turned = lax.ppermute(turned, "tm", [(0, 2), (3, 1), (1, 0), (2, 3)])
    passed = lax.ppermute(near, "tm", [(0, 1), (3, 2)])
    passed = jnp.where(inner, passed.astype(jnp.float32), 0.0)
    middle = lax.ppermute(near, "tm", [(1, 2), (2, 1)])
    later = (later.astype(jnp.float32) + passed).astype(jnp.bfloat16)
    last = lax.ppermute(later, "tm", [(0, 1), (3, 2), (1, 3), (2, 0)])
    total = own.astype(jnp.float32) + turned.astype(jnp.float32) + last.astype(jnp.float32)
    total = total + jnp.where(inner, middle.astype(jnp.float32), 0.0)
    return jnp.transpose((total / segments).astype(jnp.bfloat16), (1, 0, 2))


def solution(mesh):
    shape = tuple(SIZES[a] for a in PAIR_AXES) + (mesh.shape["tm"],)
    fine = Mesh(mesh.devices.reshape(shape), PAIR_AXES + ("tm",))
    in_specs = (P("tm", PAIR_AXES, None), P(PAIR_AXES), P(PAIR_AXES))
    out_specs = P("tm", PAIR_AXES, None)
    return jax.shard_map(local, mesh=fine, in_specs=in_specs, out_specs=out_specs, check_vma=False)
```

```python
import jax
import jax.numpy as jnp
from jax import lax
from jax.experimental import pallas as pl
from jax.experimental.pallas import tpu as pltpu
from jax.sharding import Mesh, PartitionSpec as P

LAGS = 512
NBLK = 2
PAIR_AXES = ("x", "z", "yh", "core")
SIZES = {"x": 4, "z": 8, "yh": 2, "core": 2}
MiB = 1 << 20
SENDS = ((3, 2, 1, 0), (2, 0, 3, 1), (1, 3, 0, 2), (0, 1, 2, 3))
SMEM = pl.BlockSpec(memory_space=pltpu.SMEM)
VMEM = pl.BlockSpec(memory_space=pltpu.VMEM)


def normalize_kernel(records_ref, alive_ref, out_ref, copies_ref):
    data = records_ref[0].astype(jnp.float32)
    power = jnp.mean(data * data, axis=-1, keepdims=True)
    row = lax.broadcasted_iota(jnp.int32, power.shape, 0)
    alive = jnp.zeros(power.shape, jnp.float32)
    for c in range(data.shape[0]):
        alive = jnp.where(row == c, alive_ref[c].astype(jnp.float32), alive)
    normal = (data * lax.rsqrt(power + 1e-05) * alive).astype(jnp.bfloat16)
    out_ref[...] = normal
    for i in range(copies_ref.shape[0]):
        copies_ref[i] = normal


def normalize(records, alive, copies):
    _, rows, samples = records.shape
    return pl.pallas_call(
        normalize_kernel,
        out_shape=[
            jax.ShapeDtypeStruct((rows, samples), jnp.bfloat16),
            jax.ShapeDtypeStruct((copies, rows, samples), jnp.bfloat16),
        ],
        in_specs=[VMEM, SMEM],
        out_specs=[VMEM, VMEM],
        name="normalize",
    )(records, alive)


def correlate_kernel(rows, where_ref, own_ref, mine_ref, other_ref, *rest):
    out_ref, line_ref, skew_ref, cols_ref = rest
    samples = own_ref.shape[1]
    chunk = skew_ref.shape[0] // rows
    cols = cols_ref.shape[0]
    half = cols // 2
    last = LAGS // chunk - 1
    block, core = where_ref[0], where_ref[1]
    start = pl.multiple_of(chunk * (last - where_ref[2]), chunk)
    line_ref[...] = jnp.zeros(line_ref.shape, jnp.float32)
    line_ref[:, pl.ds(2 * chunk, samples)] = own_ref[...].astype(jnp.float32)
    for c in range(rows):
        line = line_ref[pl.ds(c, 1), pl.ds(start, samples + chunk)]
        grid = jnp.broadcast_to(line, (chunk, samples + chunk))
        skewed = pltpu.roll(grid, 0, 1, stride=1, stride_axis=0)
        skew_ref[pl.ds(c * chunk, chunk), :] = skewed[:, chunk:].astype(jnp.bfloat16)
    first = block * half
    group = 2 * rows
    upper = lax.broadcasted_iota(jnp.int32, (group, samples), 0) < rows
    for at in range(0, half, 2 * group):
        here = pl.ds(pl.multiple_of(first + at, 2 * group), 2 * group)
        near, far = mine_ref[here, :].astype(jnp.float32), other_ref[here, :].astype(jnp.float32)
        even, odd = jnp.where(core == 0, near, far), jnp.where(core == 0, far, near)
        woven = []
        for part in range(2):
            e, o = even[part * group : (part + 1) * group], odd[part * group : (part + 1) * group]
            woven += [jnp.where(upper, e, pltpu.roll(o, rows, 0)), jnp.where(upper, pltpu.roll(e, rows, 0), o)]
        cols_ref[pl.ds(2 * at, 4 * group), :] = jnp.concatenate(woven, axis=0).astype(jnp.bfloat16)
    total = lax.dot_general(
        skew_ref[...], cols_ref[...], (((1,), (1,)), ((), ())), preferred_element_type=jnp.float32
    )
    out_ref[...] = total.astype(jnp.bfloat16).reshape(out_ref.shape)


def correlate(where, segments, own, mine, other):
    rows, samples = own.shape
    chunk = LAGS // segments
    cols = 2 * mine.shape[0] // NBLK
    return pl.pallas_call(
        lambda *refs: correlate_kernel(rows, *refs),
        out_shape=jax.ShapeDtypeStruct((rows, chunk, cols), jnp.bfloat16),
        in_specs=[SMEM, VMEM, VMEM, VMEM],
        out_specs=VMEM,
        scratch_shapes=[
            pltpu.VMEM((rows, samples + LAGS), jnp.float32),
            pltpu.VMEM((rows * chunk, samples), jnp.bfloat16),
            pltpu.VMEM((cols, samples), jnp.bfloat16),
        ],
        compiler_params=pltpu.CompilerParams(vmem_limit_bytes=16 * MiB),
        cost_estimate=pl.CostEstimate(
            flops=2 * rows * chunk * samples * cols, bytes_accessed=4 * MiB, transcendentals=0
        ),
        name="correlate",
    )(where, own, mine, other)


def local(records, alive, tile_block):
    segments = lax.axis_size("tm")
    core, seg = lax.axis_index("core"), lax.axis_index("tm")
    normal, sent = normalize(records, alive, SIZES["z"] * SIZES["yh"])
    slab = lax.all_to_all(sent, ("z", "yh"), 0, 0, tiled=True).reshape(-1, sent.shape[2])
    sent = jnp.broadcast_to(slab[None], (SIZES["x"],) + slab.shape)
    share = lax.all_to_all(sent, "x", 0, 0, tiled=True).reshape(-1, slab.shape[1])
    other = lax.ppermute(share, "core", [(0, 1), (1, 0)])
    sends = []
    for column in zip(*SENDS):
        value = column[-1]
        for i in reversed(range(segments - 1)):
            value = jnp.where(seg == i, column[i], value)
        sends.append(value)
    near, turned, later, own = (
        correlate(jnp.stack([tile_block[0], core, owner]).astype(jnp.int32), segments, normal, share, other)
        for owner in sends
    )
    inner = (seg == 1) | (seg == 2)
    turned = lax.ppermute(turned, "tm", [(0, 2), (3, 1), (1, 0), (2, 3)])
    passed = lax.ppermute(near, "tm", [(0, 1), (3, 2)])
    passed = jnp.where(inner, passed.astype(jnp.float32), 0.0)
    middle = lax.ppermute(near, "tm", [(1, 2), (2, 1)])
    later = (later.astype(jnp.float32) + passed).astype(jnp.bfloat16)
    last = lax.ppermute(later, "tm", [(0, 1), (3, 2), (1, 3), (2, 0)])
    total = own.astype(jnp.float32) + turned.astype(jnp.float32) + last.astype(jnp.float32)
    total = total + jnp.where(inner, middle.astype(jnp.float32), 0.0)
    return jnp.transpose((total / segments).astype(jnp.bfloat16), (1, 0, 2))


def solution(mesh):
    shape = tuple(SIZES[a] for a in PAIR_AXES) + (mesh.shape["tm"],)
    fine = Mesh(mesh.devices.reshape(shape), PAIR_AXES + ("tm",))
    in_specs = (P("tm", PAIR_AXES, None), P(PAIR_AXES), P(PAIR_AXES))
    out_specs = P("tm", PAIR_AXES, None)
    return jax.shard_map(local, mesh=fine, in_specs=in_specs, out_specs=out_specs, check_vma=False)
```

```python
import jax
import jax.numpy as jnp
from jax import lax
from jax.experimental import pallas as pl
from jax.experimental.pallas import tpu as pltpu
from jax.sharding import Mesh, PartitionSpec as P

LAGS = 512
NBLK = 2
PAIR_AXES = ("x", "z", "yh", "core")
SIZES = {"x": 4, "z": 8, "yh": 2, "core": 2}
MiB = 1 << 20
SENDS = ((3, 2, 1, 0), (2, 0, 3, 1), (1, 3, 0, 2), (0, 1, 2, 3))
SMEM = pl.BlockSpec(memory_space=pltpu.SMEM)
VMEM = pl.BlockSpec(memory_space=pltpu.VMEM)


def normalize_kernel(records_ref, alive_ref, out_ref, copies_ref):
    data = records_ref[0].astype(jnp.float32)
    power = jnp.mean(data * data, axis=-1, keepdims=True)
    row = lax.broadcasted_iota(jnp.int32, power.shape, 0)
    alive = jnp.zeros(power.shape, jnp.float32)
    for c in range(data.shape[0]):
        alive = jnp.where(row == c, alive_ref[c].astype(jnp.float32), alive)
    normal = (data * lax.rsqrt(power + 1e-05) * alive).astype(jnp.bfloat16)
    out_ref[...] = normal
    for i in range(copies_ref.shape[0]):
        copies_ref[i] = normal


def normalize(records, alive, copies):
    _, rows, samples = records.shape
    return pl.pallas_call(
        normalize_kernel,
        out_shape=[
            jax.ShapeDtypeStruct((rows, samples), jnp.bfloat16),
            jax.ShapeDtypeStruct((copies, rows, samples), jnp.bfloat16),
        ],
        in_specs=[VMEM, SMEM],
        out_specs=[VMEM, VMEM],
        name="normalize",
    )(records, alive)


def correlate_kernel(rows, where_ref, own_ref, mine_ref, other_ref, *rest):
    out_ref, line_ref, skew_ref, cols_ref = rest
    samples = own_ref.shape[1]
    chunk = skew_ref.shape[0] // rows
    cols = cols_ref.shape[0]
    half = cols // 2
    last = LAGS // chunk - 1
    block, core = where_ref[0], where_ref[1]
    start = pl.multiple_of(chunk * (last - where_ref[2]), chunk)
    for edge in (0, 2 * chunk + samples):
        line_ref[:, pl.ds(edge, 2 * chunk)] = jnp.zeros((rows, 2 * chunk), jnp.float32)
    line_ref[:, pl.ds(2 * chunk, samples)] = own_ref[...].astype(jnp.float32)
    for c in range(rows):
        line = line_ref[pl.ds(c, 1), pl.ds(start, samples + chunk)]
        grid = jnp.broadcast_to(line, (chunk, samples + chunk))
        skewed = pltpu.roll(grid, 0, 1, stride=1, stride_axis=0)
        skew_ref[pl.ds(c * chunk, chunk), :] = skewed[:, chunk:].astype(jnp.bfloat16)
    first = block * half
    group = 2 * rows
    upper = lax.broadcasted_iota(jnp.int32, (group, samples), 0) < rows
    for at in range(0, half, 2 * group):
        here = pl.ds(pl.multiple_of(first + at, 2 * group), 2 * group)
        near, far = mine_ref[here, :].astype(jnp.float32), other_ref[here, :].astype(jnp.float32)
        even, odd = jnp.where(core == 0, near, far), jnp.where(core == 0, far, near)
        woven = []
        for part in range(2):
            e, o = even[part * group : (part + 1) * group], odd[part * group : (part + 1) * group]
            woven += [jnp.where(upper, e, pltpu.roll(o, rows, 0)), jnp.where(upper, pltpu.roll(e, rows, 0), o)]
        cols_ref[pl.ds(2 * at, 4 * group), :] = jnp.concatenate(woven, axis=0).astype(jnp.bfloat16)
    total = lax.dot_general(
        skew_ref[...], cols_ref[...], (((1,), (1,)), ((), ())), preferred_element_type=jnp.float32
    )
    out_ref[...] = total.astype(jnp.bfloat16).reshape(out_ref.shape)


def correlate(where, segments, own, mine, other):
    rows, samples = own.shape
    chunk = LAGS // segments
    cols = 2 * mine.shape[0] // NBLK
    return pl.pallas_call(
        lambda *refs: correlate_kernel(rows, *refs),
        out_shape=jax.ShapeDtypeStruct((rows, chunk, cols), jnp.bfloat16),
        in_specs=[SMEM, VMEM, VMEM, VMEM],
        out_specs=VMEM,
        scratch_shapes=[
            pltpu.VMEM((rows, samples + LAGS), jnp.float32),
            pltpu.VMEM((rows * chunk, samples), jnp.bfloat16),
            pltpu.VMEM((cols, samples), jnp.bfloat16),
        ],
        compiler_params=pltpu.CompilerParams(vmem_limit_bytes=16 * MiB),
        cost_estimate=pl.CostEstimate(
            flops=2 * rows * chunk * samples * cols, bytes_accessed=4 * MiB, transcendentals=0
        ),
        name="correlate",
    )(where, own, mine, other)


def local(records, alive, tile_block):
    segments = lax.axis_size("tm")
    core, seg = lax.axis_index("core"), lax.axis_index("tm")
    normal, sent = normalize(records, alive, SIZES["z"] * SIZES["yh"])
    slab = lax.all_to_all(sent, ("z", "yh"), 0, 0, tiled=True).reshape(-1, sent.shape[2])
    sent = jnp.broadcast_to(slab[None], (SIZES["x"],) + slab.shape)
    share = lax.all_to_all(sent, "x", 0, 0, tiled=True).reshape(-1, slab.shape[1])
    other = lax.ppermute(share, "core", [(0, 1), (1, 0)])
    sends = []
    for column in zip(*SENDS):
        value = column[-1]
        for i in reversed(range(segments - 1)):
            value = jnp.where(seg == i, column[i], value)
        sends.append(value)
    near, turned, later, own = (
        correlate(jnp.stack([tile_block[0], core, owner]).astype(jnp.int32), segments, normal, share, other)
        for owner in sends
    )
    inner = (seg == 1) | (seg == 2)
    turned = lax.ppermute(turned, "tm", [(0, 2), (3, 1), (1, 0), (2, 3)])
    passed = lax.ppermute(near, "tm", [(0, 1), (3, 2)])
    passed = jnp.where(inner, passed.astype(jnp.float32), 0.0)
    middle = lax.ppermute(near, "tm", [(1, 2), (2, 1)])
    later = (later.astype(jnp.float32) + passed).astype(jnp.bfloat16)
    last = lax.ppermute(later, "tm", [(0, 1), (3, 2), (1, 3), (2, 0)])
    total = own.astype(jnp.float32) + turned.astype(jnp.float32) + last.astype(jnp.float32)
    total = total + jnp.where(inner, middle.astype(jnp.float32), 0.0)
    return jnp.transpose((total / segments).astype(jnp.bfloat16), (1, 0, 2))


def solution(mesh):
    shape = tuple(SIZES[a] for a in PAIR_AXES) + (mesh.shape["tm"],)
    fine = Mesh(mesh.devices.reshape(shape), PAIR_AXES + ("tm",))
    in_specs = (P("tm", PAIR_AXES, None), P(PAIR_AXES), P(PAIR_AXES))
    out_specs = P("tm", PAIR_AXES, None)
    return jax.shard_map(local, mesh=fine, in_specs=in_specs, out_specs=out_specs, check_vma=False)
```
